32 devices in a mesh: dom: 32 (over z, y, x, core).
Axes of the slice: x: 2, y: 2, z: 4, core: 2. Of those that a mesh axis runs over, the one named last changes fastest.
Arguments:
- dofs_start: float32 [9, 56, 4096], P(None, None, 'dom'), may hold values from -6 to 6
- star_matrix: float32 [3, 9, 9, 4096], P(None, None, None, 'dom'), may hold values from -2 to 2
- flux_local: float32 [4, 9, 9, 4096], P(None, None, None, 'dom'), may hold values from -2 to 2
- flux_neighbour: float32 [4, 9, 9, 4096], P(None, None, None, 'dom'), may hold values from -2 to 2
- derivative: float32 [3, 56, 56], replicated, may hold values from -0.75 to 0.75
- face_project: float32 [4, 56, 21], replicated, may hold values from -0.75 to 0.75
- face_lift: float32 [4, 21, 56], replicated, may hold values from -0.625 to 0.625
- face_turn: float32 [3, 21, 21], replicated, may hold values from -1.25 to 1.25
- cluster: int32 [4096], P('dom'), may hold values from 0 to 1, as said below
- face_neighbour: int32 [4, 4096], P(None, 'dom'), may hold values from 0 to 640, as said below
- orientation: int32 [4, 4096], P(None, 'dom'), may hold values from 0 to 2
- send_list: int32 [4, 1024], P(None, 'dom'), may hold values from 0 to 511, as said below
Outputs:
- dofs_end: float32 [9, 56, 4096], P(None, None, 'dom')
The draws below stay inside these ranges and needn't reach their ends.
Inputs may be any that keep to these rules, and one draw needn't show every extreme that they name: On each partition the elements of cluster 0 come before those of cluster 1; a partition holds 32 to 96 elements of cluster 0, and some partition exactly 96. `face_neighbour`: A code v < 512 is face v // 128 of local element v % 128; 512 + k * 32 + s is slot s of block k of the face table; 640 is the outer boundary. Face pairs are symmetric. `send_list`: each partition's row k holds 32 of its local face codes, each face in at most one slot of all rows.
All inputs are finite; a program needn't handle non-finite values.
Results may differ from the reference program's by a relative error of at most 0.0003.
Values sent between devices are 32-bit elements; how exact they have to be, the bound alone decides.
A program may use at most 64 MiB of HBM per device.

```python
import math
import jax
import jax.numpy as jnp
from jax import lax

NB = 56
NQ = 9
NF = 21
ORDER = 6
ELEM_DEV = 128
SLOT = 32
FAST_MAX = 96
ELEMS = 4096
N_DOM = 32


def mesh_tables(key):
    device_count = ELEMS // ELEM_DEV
    mesh_key = jax.random.fold_in(key, 7)
    remote = 4 * SLOT
    local_start = remote + ELEM_DEV // 4

    def one_device(device):
        shuffled = jax.random.permutation(jax.random.fold_in(mesh_key, device), 4 * ELEM_DEV).astype(jnp.int32)
        position = jnp.arange(4 * ELEM_DEV, dtype=jnp.int32)
        ghost_code = 4 * ELEM_DEV + (position // SLOT ^ 1) * SLOT + position % SLOT
        partner = jnp.clip(local_start + (position - local_start ^ 1), 0, 4 * ELEM_DEV - 1)
        local_code = shuffled[partner]
        face_code = jnp.where(position < remote, ghost_code, jnp.where(position < local_start, 4 * ELEM_DEV + 4 * SLOT, local_code))
        codes = jnp.zeros((4 * ELEM_DEV,), jnp.int32).at[shuffled].set(face_code.astype(jnp.int32))
        send_rows = shuffled[:remote].reshape(4, SLOT)
        return (codes, send_rows)
    codes, send_rows = jax.vmap(one_device)(jnp.arange(device_count, dtype=jnp.int32))
    neighbours = codes.reshape(device_count, 4, ELEM_DEV).transpose(1, 0, 2).reshape(4, device_count * ELEM_DEV)
    sending = send_rows.transpose(1, 0, 2).reshape(4, device_count * SLOT)
    return (neighbours.astype(jnp.int32), sending.astype(jnp.int32))


def draw_face_neighbour(key, part):
    return mesh_tables(key)[0]


def draw_send_list(key, part):
    return mesh_tables(key)[1]


def draw_cluster(key, part):
    device_count = ELEMS // ELEM_DEV
    count_key = jax.random.fold_in(key, 11)
    busy_key = jax.random.fold_in(key, 13)
    fast_counts = jax.random.randint(count_key, (device_count,), ELEM_DEV // 4, FAST_MAX + 1).astype(jnp.int32)
    busiest = jax.random.randint(busy_key, (), 0, device_count)
    fast_counts = fast_counts.at[busiest].set(FAST_MAX)
    local_index = jnp.arange(ELEM_DEV, dtype=jnp.int32)
    labels = (local_index[None, :] >= fast_counts[:, None]).astype(jnp.int32)
    return labels.reshape(device_count * ELEM_DEV)


def plant(result, rng, low, high):
    dims = result.shape
    place = [jax.random.randint(jax.random.fold_in(rng, axis), (), 0, dims[axis]) for axis in range(len(dims))]
    result = result.at[tuple(place)].set(low)
    longest = dims.index(max(dims))
    place[longest] = (place[longest] + 1) % dims[longest]
    return result.at[tuple(place)].set(high)


def block_levels(key, extent, cuts, low, largest):
    def one(axis_at, parts):
        heights = jax.random.uniform(jax.random.fold_in(jax.random.fold_in(key, 6), axis_at), (parts,), jnp.float32, low / len(cuts), largest / len(cuts))
        return jnp.repeat(jnp.exp(heights), extent[axis_at] // parts).reshape((-1,) + (1,) * (len(extent) - axis_at - 1))

    loudness = one(*cuts[0])
    for cut in cuts[1:]:
        loudness = loudness * one(*cut)
    return loudness


def centred(key, dims, width, reach, cuts=(), held_as=jnp.bfloat16):
    result = width * jax.random.normal(key, dims, jnp.float32)
    if cuts:
        result = result * block_levels(key, dims, cuts, -0.22, 0.18)
    return jnp.clip(result, -reach, reach).astype(held_as)


def setup_inputs(seed: int = 0) -> dict:
    keys = jax.random.split(jax.random.key(seed), 13)
    dofs_start = centred(keys[0], (NQ, NB, ELEMS), 1.0, 6.0, ((2, 32),), jnp.float32)
    star_matrix = centred(keys[1], (3, NQ, NQ, ELEMS), NQ ** -0.5, 2.0, ((3, 32),), jnp.float32)
    flux_local = centred(keys[2], (4, NQ, NQ, ELEMS), NQ ** -0.5, 2.0, ((3, 32),), jnp.float32)
    flux_neighbour = centred(keys[3], (4, NQ, NQ, ELEMS), NQ ** -0.5, 2.0, ((3, 32),), jnp.float32)
    derivative = centred(keys[4], (3, NB, NB), NB ** -0.5, 0.75, (), jnp.float32)
    face_project = centred(keys[5], (4, NB, NF), NB ** -0.5, 0.75, (), jnp.float32)
    face_lift = centred(keys[6], (4, NF, NB), (4 * NF) ** -0.5, 0.625, (), jnp.float32)
    face_turn = centred(keys[7], (3, NF, NF), NF ** -0.5, 1.25, (), jnp.float32)
    cluster = draw_cluster(jax.random.fold_in(keys[12], 71), 0)
    face_neighbour = draw_face_neighbour(jax.random.fold_in(keys[12], 71), 0)
    orientation = plant(jax.random.randint(keys[10], (4, ELEMS), 0, 3), jax.random.fold_in(keys[10], 1), 0, 2).astype(jnp.int32)
    send_list = draw_send_list(jax.random.fold_in(keys[12], 71), 0)
    return {"dofs_start": dofs_start, "star_matrix": star_matrix, "flux_local": flux_local, "flux_neighbour": flux_neighbour, "derivative": derivative, "face_project": face_project, "face_lift": face_lift, "face_turn": face_turn, "cluster": cluster, "face_neighbour": face_neighbour, "orientation": orientation, "send_list": send_list}


highest = lax.Precision.HIGHEST
time_step = 0.5
reach_offsets = (1, -1, 2, -2)


def star_apply(star_matrix, shifted):
    total = None
    for direction in range(star_matrix.shape[0]):
        for source in range(star_matrix.shape[2]):
            term = star_matrix[direction, :, source][:, None, :] * shifted[direction, source][None, :, :]
            total = term if total is None else total + term
    return total


def time_slope(current, star_matrix, derivative):
    shifted = jnp.einsum('qbe,dbc->dqce', current, derivative, precision=highest)
    return -star_apply(star_matrix, shifted)


def taylor(current, star_matrix, derivative):
    series = [current]
    for power in range(1, ORDER):
        series.append(time_slope(series[-1], star_matrix, derivative))
    return series


def integrate(series, lower, upper):
    summed = jnp.zeros_like(series[0])
    for power in range(len(series)):
        weight = (upper ** (power + 1) - lower ** (power + 1)) / math.factorial(power + 1)
        summed = summed + weight * series[power]
    return summed


def on_faces(integral, face_project):
    projected = jnp.einsum('qbe,ibf->qfie', integral, face_project, precision=highest)
    return projected.reshape(projected.shape[0], projected.shape[1], -1)


def outgoing_rows(face_values, send_list):
    picked = jnp.take(face_values, send_list.reshape(-1), axis=2)
    return picked.reshape(face_values.shape[0], face_values.shape[1], 4, -1)


def flux_apply(solver, traces):
    total = None
    for source in range(solver.shape[2]):
        term = jnp.moveaxis(solver[:, :, source], 0, 1)[:, None, :, :] * traces[source][None]
        total = term if total is None else total + term
    return total


def update(integral, face_values, received, star_matrix, flux_local, flux_neighbour, face_neighbour, orientation, derivative, face_lift, face_turn):
    shifted = jnp.einsum('qbe,dcb->dqce', integral, derivative, precision=highest)
    volume = star_apply(star_matrix, shifted)
    zero_column = jnp.zeros(face_values.shape[:2] + (1,), face_values.dtype)
    face_table = jnp.concatenate([face_values, received, zero_column], axis=2)
    outside = jnp.take(face_table, face_neighbour.reshape(-1), axis=2)
    rotated = jnp.einsum('qfn,hfg->hqgn', outside, face_turn, precision=highest)
    choose = (orientation.reshape(-1)[None, :] == jnp.arange(face_turn.shape[0], dtype=jnp.int32)[:, None]).astype(outside.dtype)
    turned = jnp.sum(rotated * choose[:, None, None, :], axis=0)
    elem_count = integral.shape[2]
    inside = face_values.reshape(face_values.shape[0], face_values.shape[1], 4, elem_count)
    turned = turned.reshape(turned.shape[0], turned.shape[1], 4, elem_count)
    fluxes = flux_apply(flux_local, inside) + flux_apply(flux_neighbour, turned)
    surface = jnp.einsum('pfie,ifb->pbe', fluxes, face_lift, precision=highest)
    return volume - surface


def split_parts(values):
    shaped = values.reshape(values.shape[:-1] + (N_DOM, values.shape[-1] // N_DOM))
    return jnp.moveaxis(shaped, -2, 0)


def join_parts(values):
    moved = jnp.moveaxis(values, 0, -2)
    return moved.reshape(moved.shape[:-2] + (-1,))


def deliver(outgoing):
    blocks = [jnp.roll(outgoing[:, :, :, direction], reach_offsets[direction], axis=0) for direction in range(4)]
    stacked = jnp.stack(blocks, axis=3)
    return stacked.reshape(stacked.shape[0], stacked.shape[1], stacked.shape[2], -1)


def reference(dofs_start, star_matrix, flux_local, flux_neighbour, derivative, face_project, face_lift, face_turn, cluster, face_neighbour, orientation, send_list):
    dofs_parts = split_parts(dofs_start)
    star_parts = split_parts(star_matrix)
    local_parts = split_parts(flux_local)
    neighbour_parts = split_parts(flux_neighbour)
    cluster_parts = split_parts(cluster)
    code_parts = split_parts(face_neighbour)
    turn_parts = split_parts(orientation)
    send_parts = split_parts(send_list)

    def section_one(pieces):
        current, stars, sends = pieces
        series = taylor(current, stars, derivative)
        first_half = integrate(series, 0.0, time_step)
        late_half = integrate(series, time_step, 2.0 * time_step)
        return first_half, late_half, outgoing_rows(on_faces(first_half, face_project), sends)

    first_half, late_half, outgoing = lax.map(section_one, (dofs_parts, star_parts, send_parts))
    received = deliver(outgoing)

    def section_two(pieces):
        current, stars, fl_local, fl_neigh, clusters, codes, turns, sends, first_part, late_part, arrived = pieces
        middle = current + update(first_part, on_faces(first_part, face_project), arrived, stars, fl_local, fl_neigh, codes, turns, derivative, face_lift, face_turn)
        fresh = integrate(taylor(middle, stars, derivative), 0.0, time_step)
        second_half = jnp.where((clusters == 0)[None, None, :], fresh, late_part)
        return middle, second_half, outgoing_rows(on_faces(second_half, face_project), sends)

    middle, second_half, outgoing = lax.map(section_two, (dofs_parts, star_parts, local_parts, neighbour_parts, cluster_parts, code_parts, turn_parts, send_parts, first_half, late_half, received))
    received = deliver(outgoing)

    def section_three(pieces):
        mid_part, stars, fl_local, fl_neigh, codes, turns, second_part, arrived = pieces
        return mid_part + update(second_part, on_faces(second_part, face_project), arrived, stars, fl_local, fl_neigh, codes, turns, derivative, face_lift, face_turn)

    finished = lax.map(section_three, (middle, star_parts, local_parts, neighbour_parts, code_parts, turn_parts, second_half, received))
    return join_parts(finished)
```

```python
import functools
import math

import jax
import jax.numpy as jnp
from jax import lax
from jax.experimental import pallas as pl
from jax.experimental.pallas import tpu as pltpu
from jax.sharding import PartitionSpec as P

ORDER = 6
time_step = 0.5
reach_offsets = (1, -1, 2, -2)
MESH = pl.DeviceIdType.MESH
LANES = 128
f32, bf16 = jnp.float32, jnp.bfloat16
groups = ((0, 1, 2, 3), (4, 5, 6, 7), (8,))


def weight(power, lower, upper):
    return (upper ** (power + 1) - lower ** (power + 1)) / math.factorial(power + 1)


def split(x):
    high = x.astype(bf16)
    return high, (x - high.astype(f32)).astype(bf16)


def stacked(x):
    high, low = split(x)
    return jnp.concatenate([high, high, low], axis=0)


def place(pieces, blocks):
    out = []
    for block in range(blocks):
        total = None
        for x, offset, width in pieces:
            if offset >= (block + 1) * LANES or offset + width <= block * LANES:
                continue
            moved = pltpu.roll(x, offset % LANES, axis=1) if offset % LANES else x
            lane = lax.broadcasted_iota(jnp.int32, x.shape, 1) + block * LANES
            moved = jnp.where((lane >= offset) & (lane < offset + width), moved, 0.0)
            total = moved if total is None else total + moved
        out.append(total)
    return out[0] if blocks == 1 else jnp.concatenate(out, axis=1)


def three(x, width):
    high = x.astype(bf16).astype(f32)
    low = x - high
    blocks = -(-3 * width // LANES)
    whole = place([(high, 0, width), (low, width, width), (high, 2 * width, width)], blocks)
    return whole.astype(bf16)


def pad_rows(x, rows):
    if x.shape[0] == rows:
        return x
    return jnp.concatenate([x, jnp.zeros((rows - x.shape[0], x.shape[1]), x.dtype)], axis=0)


def kernel(
    peers,
    dofs, star, flux_l, flux_n, deriv, proj, lift, turn, cluster, codes, orient, sends,
    out,
    square, a_slope, a_vol, a_proj, a_lift, a_turn,
    hot, hot_send, code_row,
    shifted, integral, late, faces, table, outside, turned, fluxes, sent, got,
    send_sem, recv_sem,
):
    me = lax.axis_index("dom")
    nq, nb, ne = dofs.shape
    nf = proj.shape[2]
    slot = sends.shape[1]
    fr = 24
    kb = 64

    barrier = pltpu.get_barrier_semaphore()
    for offset in reach_offsets:
        pl.semaphore_signal(
            barrier, inc=1, device_id=(lax.rem(me + offset + peers, peers),), device_id_type=MESH
        )

    square[...] = jnp.zeros_like(square)
    for d in range(3):
        square[0:nb, 0:nb] = deriv[d]
        a_vol[d * nb:(d + 1) * nb, :] = three(square[0:nb, :], kb)[:, :3 * kb].astype(f32)
        flipped = -jnp.transpose(square[...])
        a_slope[d * nb:(d + 1) * nb, :] = three(flipped[0:nb, :], kb)[:, :3 * kb].astype(f32)
    square[...] = jnp.zeros_like(square)
    for i in range(4):
        square[0:nb, 0:nf] = proj[i]
        flipped = jnp.transpose(square[...])
        a_proj[i * fr:(i + 1) * fr, :] = three(flipped[0:fr, :], kb)[:, :3 * kb].astype(f32)
    square[...] = jnp.zeros_like(square)
    for i in range(4):
        square[i * fr:i * fr + nf, 0:nb] = lift[i]
    flipped = jnp.transpose(square[...])
    a_lift[...] = three(flipped[0:nb, :], 4 * fr)[:, :12 * fr].astype(f32)
    square[...] = jnp.zeros_like(square)
    for h in range(3):
        square[0:nf, 0:nf] = turn[h]
        flipped = jnp.transpose(square[...])
        a_turn[h * fr:(h + 1) * fr, :] = three(flipped[0:fr, :], 32)[:, :96].astype(f32)

    for i in range(4):
        for start in range(0, 640, 128):
            number = lax.broadcasted_iota(jnp.int32, (128, ne), 0) + start
            same = number == codes[i:i + 1, :]
            hot[start:start + 128, i * ne:(i + 1) * ne] = jnp.where(same, 1.0, 0.0).astype(bf16)
    code_row[...] = jnp.zeros_like(code_row)
    code_row[0:4, 0:slot] = sends[...]
    wanted = code_row[0:1, :]
    for k in range(1, 4):
        wanted = wanted + pltpu.roll(code_row[...], k * slot, axis=1)[k:k + 1, :]
    for start in range(0, 512, 128):
        number = lax.broadcasted_iota(jnp.int32, (128, ne), 0) + start
        hot_send[start:start + 128, :] = jnp.where(number == wanted, 1.0, 0.0).astype(bf16)

    table[...] = jnp.zeros_like(table)
    for q in range(nq):
        out[q] = dofs[q]

    def products(lhs, values, emit):
        at = 0
        while at < len(values):
            pair = values[at:at + 2]
            rhs = [stacked(pad_rows(v, kb)) for v in pair]
            rhs = rhs[0] if len(rhs) == 1 else jnp.concatenate(rhs, axis=1)
            got_ = jnp.dot(lhs, rhs, preferred_element_type=f32)
            for j in range(len(pair)):
                emit(at + j, got_[:, j * LANES:(j + 1) * LANES])
            at += 2

    def star_apply(buffer, ps):
        acc = [None] * len(ps)
        for q in range(nq):
            for d in range(3):
                s = shifted[buffer, q, d * nb:(d + 1) * nb, :]
                for j, p in enumerate(ps):
                    term = star[d, p, q:q + 1, :] * s
                    acc[j] = term if acc[j] is None else acc[j] + term
        return acc

    lane = lax.broadcasted_iota(jnp.int32, (nb, LANES), 1)

    def stage(s, carry):
        slope_lhs = a_slope[...].astype(bf16)

        def keep(buffer, first):
            def emit(index, product):
                shifted[buffer, first + index] = product
            return emit

        for ps in groups:
            values = [out[p] for p in ps]
            for p, v in zip(ps, values):
                integral[p] = weight(0, 0.0, time_step) * v
                late[s, p] = weight(0, time_step, 2 * time_step) * v
            products(slope_lhs, values, keep(0, ps[0]))
        for power in range(1, ORDER):
            buffer = (power - 1) % 2
            for ps in groups:
                values = star_apply(buffer, ps)
                for p, v in zip(ps, values):
                    integral[p] += weight(power, 0.0, time_step) * v
                    late[s, p] += weight(power, time_step, 2 * time_step) * v
                if power < ORDER - 1:
                    products(slope_lhs, values, keep(1 - buffer, ps[0]))

        slow = (jnp.broadcast_to(cluster[...], (nb, LANES)) != 0) & (s == 1)
        values = []
        for q in range(nq):
            values.append(jnp.where(slow, late[0, q], integral[q]))

        def emit_faces(q, product):
            faces[q] = product
            for i in range(4):
                table[q * fr:(q + 1) * fr, i * ne:(i + 1) * ne] = product[i * fr:(i + 1) * fr]
        products(a_proj[...].astype(bf16), values, emit_faces)

        high, low = split(table[:, 0:4 * ne])
        chosen = jnp.dot(high, hot_send[...], preferred_element_type=f32) + jnp.dot(
            low, hot_send[...], preferred_element_type=f32
        )
        for k in range(4):
            packed = None
            for j in range(4):
                rows = chosen[j * nb:(j + 1) * nb]
                shift = ((j - k) % 4) * slot
                rows = pltpu.roll(rows, shift, axis=1) if shift else rows
                packed = rows if packed is None else jnp.where(lane >= j * slot, rows, packed)
            sent[s, k] = packed

        @pl.when(s == 0)
        def _():
            pl.semaphore_wait(barrier, 4)

        copies = []
        for k, offset in enumerate(reach_offsets):
            copy = pltpu.make_async_remote_copy(
                src_ref=sent.at[s, k],
                dst_ref=got.at[s, k],
                send_sem=send_sem.at[s, k],
                recv_sem=recv_sem.at[s, k],
                device_id=(lax.rem(me + offset + peers, peers),),
                device_id_type=MESH,
            )
            copy.start()
            copies.append(copy)

        products(a_vol[...].astype(bf16), values, keep(0, 0))
        outside[...] = jnp.dot(high, hot[0:4 * ne, :], preferred_element_type=f32) + jnp.dot(
            low, hot[0:4 * ne, :], preferred_element_type=f32
        )
        for ps in groups:
            for p, v in zip(ps, star_apply(0, ps)):
                out[p] += v
        for i in range(4):
            acc = [None] * nq
            for q in range(nq):
                trace = faces[q, i * fr:(i + 1) * fr, :]
                for p in range(nq):
                    term = flux_l[i, p, q:q + 1, :] * trace
                    acc[p] = term if acc[p] is None else acc[p] + term
            for p in range(nq):
                fluxes[p, i * fr:(i + 1) * fr, :] = acc[p]

        for copy in copies:
            copy.wait()
        for j in range(4):
            rows = None
            for k in range(4):
                block = got[s, k]
                shift = ((k - j) % 4) * slot
                block = pltpu.roll(block, shift, axis=1) if shift else block
                rows = block if rows is None else jnp.where(lane >= k * slot, block, rows)
            table[j * nb:(j + 1) * nb, 4 * ne:5 * ne] = rows
        high, low = split(table[:, 4 * ne:5 * ne])
        outside[...] += jnp.dot(high, hot[4 * ne:5 * ne, :], preferred_element_type=f32) + jnp.dot(
            low, hot[4 * ne:5 * ne, :], preferred_element_type=f32
        )

        turn_lhs = a_turn[...].astype(bf16)
        for q in range(nq):
            rhs = stacked(pad_rows(outside[q * fr:(q + 1) * fr, :], 32))
            product = jnp.dot(turn_lhs, rhs, preferred_element_type=f32)
            for i in range(4):
                which = jnp.broadcast_to(orient[i:i + 1, :], (fr, LANES))
                h0, h1, h2 = (
                    product[h * fr:(h + 1) * fr, i * ne:(i + 1) * ne] for h in range(3)
                )
                turned[q, i * fr:(i + 1) * fr, :] = jnp.where(
                    which == 0, h0, jnp.where(which == 1, h1, h2)
                )
        for i in range(4):
            acc = [fluxes[p, i * fr:(i + 1) * fr, :] for p in range(nq)]
            for q in range(nq):
                trace = turned[q, i * fr:(i + 1) * fr, :]
                for p in range(nq):
                    acc[p] = acc[p] + flux_n[i, p, q:q + 1, :] * trace
            for p in range(nq):
                fluxes[p, i * fr:(i + 1) * fr, :] = acc[p]
        lift_lhs = a_lift[...].astype(bf16)
        for at in range(0, nq, 2):
            pair = list(range(at, min(at + 2, nq)))
            rhs = [stacked(fluxes[p]) for p in pair]
            rhs = rhs[0] if len(rhs) == 1 else jnp.concatenate(rhs, axis=1)
            surface = jnp.dot(lift_lhs, rhs, preferred_element_type=f32)
            for j, p in enumerate(pair):
                out[p] -= surface[:, j * LANES:(j + 1) * LANES]
        return carry

    lax.fori_loop(0, 2, stage, 0)


def per_device(*args):
    peers = lax.axis_size("dom")
    dofs = args[0]
    nq, nb, ne = dofs.shape
    cluster = args[8].reshape(1, ne)
    args = args[:8] + (cluster,) + args[9:]
    vmem = pl.BlockSpec(memory_space=pltpu.VMEM)
    return pl.pallas_call(
        functools.partial(kernel, peers),
        out_shape=jax.ShapeDtypeStruct(dofs.shape, dofs.dtype),
        in_specs=[vmem] * 12,
        out_specs=vmem,
        scratch_shapes=[
            pltpu.VMEM((128, 128), f32),
            pltpu.VMEM((168, 192), f32),
            pltpu.VMEM((168, 192), f32),
            pltpu.VMEM((96, 192), f32),
            pltpu.VMEM((56, 288), f32),
            pltpu.VMEM((72, 96), f32),
            pltpu.VMEM((640, 512), bf16),
            pltpu.VMEM((512, 128), bf16),
            pltpu.VMEM((8, 128), jnp.int32),
            pltpu.VMEM((2, 9, 168, 128), f32),
            pltpu.VMEM((9, 56, 128), f32),
            pltpu.VMEM((2, 9, 56, 128), f32),
            pltpu.VMEM((9, 96, 128), f32),
            pltpu.VMEM((224, 640), f32),
            pltpu.VMEM((224, 512), f32),
            pltpu.VMEM((9, 96, 128), f32),
            pltpu.VMEM((9, 96, 128), f32),
            pltpu.VMEM((2, 4, 56, 128), f32),
            pltpu.VMEM((2, 4, 56, 128), f32),
            pltpu.SemaphoreType.DMA((2, 4)),
            pltpu.SemaphoreType.DMA((2, 4)),
        ],
        compiler_params=pltpu.CompilerParams(
            collective_id=0, has_side_effects=True, vmem_limit_bytes=40 * 1024 * 1024
        ),
        cost_estimate=pl.CostEstimate(
            flops=400_000_000, bytes_accessed=2_000_000, transcendentals=0
        ),
    )(*args)


def solution(mesh):
    return jax.shard_map(
        per_device,
        mesh=mesh,
        in_specs=(
            P(None, None, "dom"),
            P(None, None, None, "dom"),
            P(None, None, None, "dom"),
            P(None, None, None, "dom"),
            P(),
            P(),
            P(),
            P(),
            P("dom"),
            P(None, "dom"),
            P(None, "dom"),
            P(None, "dom"),
        ),
        out_specs=P(None, None, "dom"),
        check_vma=False,
    )
```

```python
import functools
import math

import jax
import jax.numpy as jnp
from jax import lax
from jax.experimental import pallas as pl
from jax.experimental.pallas import tpu as pltpu
from jax.sharding import PartitionSpec as P

ORDER = 6
time_step = 0.5
reach_offsets = (1, -1, 2, -2)
MESH = pl.DeviceIdType.MESH
LANES = 128
f32, bf16 = jnp.float32, jnp.bfloat16
groups = ((0, 1, 2, 3), (4, 5, 6, 7), (8,))


def weight(power, lower, upper):
    return (upper ** (power + 1) - lower ** (power + 1)) / math.factorial(power + 1)


def split(x):
    high = x.astype(bf16)
    return high, (x - high.astype(f32)).astype(bf16)


def stacked(x):
    high, low = split(x)
    return jnp.concatenate([high, high, low], axis=0)


def place(pieces, blocks):
    out = []
    for block in range(blocks):
        total = None
        for x, offset, width in pieces:
            if offset >= (block + 1) * LANES or offset + width <= block * LANES:
                continue
            moved = pltpu.roll(x, offset % LANES, axis=1) if offset % LANES else x
            lane = lax.broadcasted_iota(jnp.int32, x.shape, 1) + block * LANES
            moved = jnp.where((lane >= offset) & (lane < offset + width), moved, 0.0)
            total = moved if total is None else total + moved
        out.append(total)
    return out[0] if blocks == 1 else jnp.concatenate(out, axis=1)


def three(x, width):
    high = x.astype(bf16).astype(f32)
    low = x - high
    blocks = -(-3 * width // LANES)
    whole = place([(high, 0, width), (low, width, width), (high, 2 * width, width)], blocks)
    return whole.astype(bf16)


def pad_rows(x, rows):
    if x.shape[0] == rows:
        return x
    return jnp.concatenate([x, jnp.zeros((rows - x.shape[0], x.shape[1]), x.dtype)], axis=0)


def kernel(
    peers,
    *refs,
):
    far, out, near, loaded = refs[:12], refs[12], refs[13:25], refs[25]
    run(peers, far, near, loaded, *near, out, *refs[26:])


def run(
    peers, far, near, loaded,
    dofs, star, flux_l, flux_n, deriv, proj, lift, turn, cluster, codes, orient, sends,
    out,
    square, a_slope, a_vol, a_proj, a_lift, a_turn,
    hot, hot_send, code_row,
    shifted, integral, late, faces, table, outside, turned, fluxes, sent, got,
    send_sem, recv_sem,
):
    me = lax.axis_index("dom")
    nq, nb, ne = dofs.shape
    nf = proj.shape[0]
    slot = sends.shape[1]
    fr = 24
    kb = 64

    barrier = pltpu.get_barrier_semaphore()
    for offset in reach_offsets:
        pl.semaphore_signal(
            barrier, inc=1, device_id=(lax.rem(me + offset + peers, peers),), device_id_type=MESH
        )

    loads = [pltpu.make_async_copy(far[n], near[n], loaded.at[n]) for n in range(12)]
    for n in (4, 5, 6, 7, 8, 9, 10, 11, 0, 1, 2, 3):
        loads[n].start()
    for n in range(4, 12):
        loads[n].wait()

    square[...] = jnp.zeros_like(square)
    for d in range(3):
        row = (d % 2) * kb
        square[row:row + nb, 0:nb] = deriv[d]
        a_vol[d * nb:(d + 1) * nb, :] = three(square[row:row + nb, :], kb)[:, :3 * kb].astype(f32)
        if d == 0:
            continue
        flipped = -jnp.transpose(square[...])
        for e in ((0, 1) if d == 1 else (2,)):
            part = flipped[0:nb, :]
            part = pltpu.roll(part, kb, axis=1) if e % 2 else part
            a_slope[e * nb:(e + 1) * nb, :] = three(part, kb)[:, :3 * kb].astype(f32)
    square[...] = jnp.zeros_like(square)
    for i in range(4):
        square[0:nf, 0:nb] = proj[:, i, :]
        a_proj[i * fr:(i + 1) * fr, :] = three(square[0:fr, :], kb)[:, :3 * kb].astype(f32)
    square[...] = jnp.zeros_like(square)
    for i in range(4):
        square[i * fr:i * fr + nf, 0:nb] = lift[:, i, :]
    flipped = jnp.transpose(square[...])
    a_lift[...] = three(flipped[0:nb, :], 4 * fr)[:, :12 * fr].astype(f32)
    square[...] = jnp.zeros_like(square)
    for h in range(3):
        square[h * 32:h * 32 + nf, 0:nf] = turn[h]
    flipped = jnp.transpose(square[...])[0:fr, :]
    for h in range(3):
        part = pltpu.roll(flipped, LANES - h * 32, axis=1) if h else flipped
        a_turn[h * fr:(h + 1) * fr, :] = three(part, 32)[:, :96].astype(f32)

    for i in range(4):
        for start in range(0, 640, 128):
            number = lax.broadcasted_iota(jnp.int32, (128, ne), 0) + start
            same = number == codes[i:i + 1, :]
            hot[start:start + 128, i * ne:(i + 1) * ne] = jnp.where(same, 1.0, 0.0).astype(bf16)
    code_row[...] = jnp.zeros_like(code_row)
    code_row[0:4, 0:slot] = sends[...]
    wanted = code_row[0:1, :]
    for k in range(1, 4):
        wanted = wanted + pltpu.roll(code_row[...], k * slot, axis=1)[k:k + 1, :]
    for start in range(0, 512, 128):
        number = lax.broadcasted_iota(jnp.int32, (128, ne), 0) + start
        hot_send[start:start + 128, :] = jnp.where(number == wanted, 1.0, 0.0).astype(bf16)

    table[...] = jnp.zeros_like(table)
    loads[0].wait()
    loads[1].wait()
    for q in range(nq):
        out[q] = dofs[q]

    def products(lhs, values, emit):
        at = 0
        while at < len(values):
            pair = values[at:at + 2]
            rhs = [stacked(pad_rows(v, kb)) for v in pair]
            rhs = rhs[0] if len(rhs) == 1 else jnp.concatenate(rhs, axis=1)
            got_ = jnp.dot(lhs, rhs, preferred_element_type=f32)
            for j in range(len(pair)):
                emit(at + j, got_[:, j * LANES:(j + 1) * LANES])
            at += 2

    def star_apply(buffer, ps):
        acc = [None] * len(ps)
        for q in range(nq):
            for d in range(3):
                s = shifted[buffer, q, d * nb:(d + 1) * nb, :]
                for j, p in enumerate(ps):
                    term = star[p, q, d:d + 1, :] * s
                    acc[j] = term if acc[j] is None else acc[j] + term
        return acc

    lane = lax.broadcasted_iota(jnp.int32, (nb, LANES), 1)

    def stage(s, carry):
        slope_lhs = a_slope[...].astype(bf16)

        def keep(buffer, first):
            def emit(index, product):
                shifted[buffer, first + index] = product
            return emit

        for ps in groups:
            values = [out[p] for p in ps]
            for p, v in zip(ps, values):
                integral[p] = weight(0, 0.0, time_step) * v
                late[s, p] = weight(0, time_step, 2 * time_step) * v
            products(slope_lhs, values, keep(0, ps[0]))
        for power in range(1, ORDER):
            buffer = (power - 1) % 2
            for ps in groups:
                values = star_apply(buffer, ps)
                for p, v in zip(ps, values):
                    integral[p] += weight(power, 0.0, time_step) * v
                    late[s, p] += weight(power, time_step, 2 * time_step) * v
                if power < ORDER - 1:
                    products(slope_lhs, values, keep(1 - buffer, ps[0]))

        slow = (jnp.broadcast_to(cluster[...], (nb, LANES)) != 0) & (s == 1)
        values = []
        for q in range(nq):
            values.append(jnp.where(slow, late[0, q], integral[q]))

        def emit_faces(q, product):
            faces[q] = product
            for i in range(4):
                table[q * fr:(q + 1) * fr, i * ne:(i + 1) * ne] = product[i * fr:(i + 1) * fr]
        products(a_proj[...].astype(bf16), values, emit_faces)

        high, low = split(table[:, 0:4 * ne])
        chosen = jnp.dot(high, hot_send[...], preferred_element_type=f32) + jnp.dot(
            low, hot_send[...], preferred_element_type=f32
        )
        for k in range(4):
            packed = None
            for j in range(4):
                rows = chosen[j * nb:(j + 1) * nb]
                shift = ((j - k) % 4) * slot
                rows = pltpu.roll(rows, shift, axis=1) if shift else rows
                packed = rows if packed is None else jnp.where(lane >= j * slot, rows, packed)
            sent[s, k] = packed

        @pl.when(s == 0)
        def _():
            loads[2].wait()
            loads[3].wait()
            pl.semaphore_wait(barrier, 4)

        copies = []
        for k, offset in enumerate(reach_offsets):
            copy = pltpu.make_async_remote_copy(
                src_ref=sent.at[s, k],
                dst_ref=got.at[s, k],
                send_sem=send_sem.at[s, k],
                recv_sem=recv_sem.at[s, k],
                device_id=(lax.rem(me + offset + peers, peers),),
                device_id_type=MESH,
            )
            copy.start()
            copies.append(copy)

        products(a_vol[...].astype(bf16), values, keep(0, 0))
        outside[...] = jnp.dot(high, hot[0:4 * ne, :], preferred_element_type=f32) + jnp.dot(
            low, hot[0:4 * ne, :], preferred_element_type=f32
        )
        for ps in groups:
            for p, v in zip(ps, star_apply(0, ps)):
                out[p] += v
        for i in range(4):
            acc = [None] * nq
            for q in range(nq):
                trace = faces[q, i * fr:(i + 1) * fr, :]
                for p in range(nq):
                    term = flux_l[p, q, i:i + 1, :] * trace
                    acc[p] = term if acc[p] is None else acc[p] + term
            for p in range(nq):
                fluxes[p, i * fr:(i + 1) * fr, :] = acc[p]

        for copy in copies:
            copy.wait()
        for j in range(4):
            rows = None
            for k in range(4):
                block = got[s, k]
                shift = ((k - j) % 4) * slot
                block = pltpu.roll(block, shift, axis=1) if shift else block
                rows = block if rows is None else jnp.where(lane >= k * slot, block, rows)
            table[j * nb:(j + 1) * nb, 4 * ne:5 * ne] = rows
        high, low = split(table[:, 4 * ne:5 * ne])
        outside[...] += jnp.dot(high, hot[4 * ne:5 * ne, :], preferred_element_type=f32) + jnp.dot(
            low, hot[4 * ne:5 * ne, :], preferred_element_type=f32
        )

        turn_lhs = a_turn[...].astype(bf16)
        for q in range(nq):
            rhs = stacked(pad_rows(outside[q * fr:(q + 1) * fr, :], 32))
            product = jnp.dot(turn_lhs, rhs, preferred_element_type=f32)
            for i in range(4):
                which = jnp.broadcast_to(orient[i:i + 1, :], (fr, LANES))
                h0, h1, h2 = (
                    product[h * fr:(h + 1) * fr, i * ne:(i + 1) * ne] for h in range(3)
                )
                turned[q, i * fr:(i + 1) * fr, :] = jnp.where(
                    which == 0, h0, jnp.where(which == 1, h1, h2)
                )
        for i in range(4):
            acc = [fluxes[p, i * fr:(i + 1) * fr, :] for p in range(nq)]
            for q in range(nq):
                trace = turned[q, i * fr:(i + 1) * fr, :]
                for p in range(nq):
                    acc[p] = acc[p] + flux_n[p, q, i:i + 1, :] * trace
            for p in range(nq):
                fluxes[p, i * fr:(i + 1) * fr, :] = acc[p]
        lift_lhs = a_lift[...].astype(bf16)
        for at in range(0, nq, 2):
            pair = list(range(at, min(at + 2, nq)))
            rhs = [stacked(fluxes[p]) for p in pair]
            rhs = rhs[0] if len(rhs) == 1 else jnp.concatenate(rhs, axis=1)
            surface = jnp.dot(lift_lhs, rhs, preferred_element_type=f32)
            for j, p in enumerate(pair):
                out[p] -= surface[:, j * LANES:(j + 1) * LANES]
        return carry

    lax.fori_loop(0, 2, stage, 0)


def per_device(*args):
    peers = lax.axis_size("dom")
    dofs = args[0]
    nq, nb, ne = dofs.shape
    cluster = args[8].reshape(1, ne)
    across = [jnp.transpose(a, (1, 2, 0, 3)) for a in args[1:4]]
    proj, lift = jnp.transpose(args[5], (2, 0, 1)), jnp.transpose(args[6], (1, 0, 2))
    args = (dofs, *across, args[4], proj, lift, args[7], cluster, *args[9:])
    vmem = pl.BlockSpec(memory_space=pltpu.VMEM)
    return pl.pallas_call(
        functools.partial(kernel, peers),
        out_shape=jax.ShapeDtypeStruct(dofs.shape, dofs.dtype),
        in_specs=[pl.BlockSpec(memory_space=pl.ANY)] * 12,
        out_specs=vmem,
        scratch_shapes=[
            *(pltpu.VMEM(a.shape, a.dtype) for a in args),
            pltpu.SemaphoreType.DMA((12,)),
            pltpu.VMEM((128, 128), f32),
            pltpu.VMEM((168, 192), f32),
            pltpu.VMEM((168, 192), f32),
            pltpu.VMEM((96, 192), f32),
            pltpu.VMEM((56, 288), f32),
            pltpu.VMEM((72, 96), f32),
            pltpu.VMEM((640, 512), bf16),
            pltpu.VMEM((512, 128), bf16),
            pltpu.VMEM((8, 128), jnp.int32),
            pltpu.VMEM((2, 9, 168, 128), f32),
            pltpu.VMEM((9, 56, 128), f32),
            pltpu.VMEM((2, 9, 56, 128), f32),
            pltpu.VMEM((9, 96, 128), f32),
            pltpu.VMEM((224, 640), f32),
            pltpu.VMEM((224, 512), f32),
            pltpu.VMEM((9, 96, 128), f32),
            pltpu.VMEM((9, 96, 128), f32),
            pltpu.VMEM((2, 4, 56, 128), f32),
            pltpu.VMEM((2, 4, 56, 128), f32),
            pltpu.SemaphoreType.DMA((2, 4)),
            pltpu.SemaphoreType.DMA((2, 4)),
        ],
        compiler_params=pltpu.CompilerParams(
            collective_id=0, has_side_effects=True, vmem_limit_bytes=60 * 1024 * 1024
        ),
        cost_estimate=pl.CostEstimate(
            flops=400_000_000, bytes_accessed=2_000_000, transcendentals=0
        ),
    )(*args)


def solution(mesh):
    return jax.shard_map(
        per_device,
        mesh=mesh,
        in_specs=(
            P(None, None, "dom"),
            P(None, None, None, "dom"),
            P(None, None, None, "dom"),
            P(None, None, None, "dom"),
            P(),
            P(),
            P(),
            P(),
            P("dom"),
            P(None, "dom"),
            P(None, "dom"),
            P(None, "dom"),
        ),
        out_specs=P(None, None, "dom"),
        check_vma=False,
    )
```
